32 devices in a mesh: pipe: 4 (over y, core), expert: 4 (over z), dp: 2 (over x).
Axes of the slice: x: 2, y: 2, z: 4, core: 2. Of those that a mesh axis runs over, the one named last changes fastest.
Arguments:
- section_grad: bfloat16 [4, 1024, 7168], P('pipe', ('expert', 'dp')), may hold values from -6 to 6
- loss_grad: bfloat16 [1024, 7168], P(('expert', 'dp')), may hold values from -6 to 6
- expert_ids: int32 [4, 1024, 8], P('pipe', ('expert', 'dp')), may hold values from 0 to 255, all different within a row
- gate_values: bfloat16 [4, 1024, 8], P('pipe', ('expert', 'dp')), may hold values from 0.049804688 to 0.59765625
- down_inputs: bfloat16 [4, 2, 16, 1024], P('pipe', 'dp', None, 'expert'), may hold values from -1.59375 to 1.59375
Outputs:
- down_grad: bfloat16 [4, 7168, 1024], P('pipe', 'dp', 'expert')
The draws below stay inside these ranges and needn't reach their ends.
Inputs may be any that keep to these rules, and one draw needn't show every extreme that they name: `expert_ids`: each row names 8 different experts; every expert is named by some row.
All inputs are finite; a program needn't handle non-finite values.
Results may differ from the reference program's by a relative error of at most 0.009.
Values may be sent and summed in bfloat16 or wider, within the bound.
A program may use at most 64 MiB of HBM per device.

```python
import jax
import jax.numpy as jnp
from jax import lax

D = 7168
ROUTED = 256
TOPK = 8
HID = 1024
TOK_DEV = 128
CAP = 4
EXPERTS = 1
GROUPS = 2
SECTIONS = 4
TOKENS = 1024
SLOTS = 16


def shard_levels(key, extent, split, least, top_value):
    factor_of, own = 1.0, jax.random.fold_in(key, 6)
    for position, blocks in split:
        heights = jnp.exp(jax.random.uniform(jax.random.fold_in(own, position), (blocks,), jnp.float32, least / len(split), top_value / len(split)))
        factor_of = factor_of * jnp.repeat(heights, extent[position] // blocks).reshape([-1 if axis == position else 1 for axis in range(len(extent))])
    return factor_of


def choose_distinct(stream_key, rows, amount, top, lift):
    sequence = jax.random.permutation(jax.random.fold_in(stream_key, 1), amount)
    boost = sequence
    for power in range(3):
        boost = boost * boost // amount
    boost = boost * lift // amount
    tickets = jax.random.randint(jax.random.fold_in(stream_key, 2), (rows, amount), 0, 4096) + boost
    holders = jax.random.permutation(jax.random.fold_in(stream_key, 3), rows)[jnp.arange(amount) % rows]
    tickets = jnp.where(jnp.arange(rows)[:, None] == holders[None, :], 1 << 14, tickets)
    score = tickets * amount + jnp.arange(amount)
    return lax.top_k(score.astype(jnp.int32), top)[1].astype(jnp.int32)


def bell_draw(stream_key, dims, scale, reach, shards=(), kind=jnp.bfloat16):
    gain = shard_levels(stream_key, dims, shards, -0.22, 0.18) if shards else 1.0
    drawn = jax.random.normal(stream_key, dims, jnp.float32) * scale * gain
    return jnp.minimum(jnp.maximum(drawn, -reach), reach).astype(kind)


def setup_inputs(seed: int = 0) -> dict:
    splits = jax.random.split(jax.random.key(seed), 6)
    return {
        "section_grad": bell_draw(splits[0], (SECTIONS, TOKENS, D), 1.0, 6.0, ((0, 4), (1, 8))),
        "loss_grad": bell_draw(splits[1], (TOKENS, D), 1.0, 6.0, ((0, 8),)),
        "expert_ids": choose_distinct(splits[2], SECTIONS * TOKENS, ROUTED, TOPK, 512).reshape((SECTIONS, TOKENS, TOPK)),
        "gate_values": jnp.clip(0.049804688 + 0.54785156 * jax.random.uniform(splits[3], (SECTIONS, TOKENS, TOPK), jnp.float32) ** shard_levels(splits[3], (SECTIONS, TOKENS, TOPK), ((0, 4), (1, 8)), -0.2, 0.2), 0.049804688, 0.59765625).astype(jnp.bfloat16),
        "down_inputs": bell_draw(splits[4], (SECTIONS, GROUPS, SLOTS, EXPERTS * HID), 0.2, 1.59375, ((0, 4), (1, 2), (3, 4))),
    }


def route_tables(id_table, gate_table):
    n_blocks = id_table.shape[0] // TOK_DEV
    flat_ids = id_table.reshape(n_blocks, TOK_DEV * TOPK)
    onehot = (flat_ids[:, :, None] == jnp.arange(EXPERTS, dtype=jnp.int32)[None, None, :]).astype(jnp.int32)
    before = jnp.cumsum(onehot, axis=1) - onehot
    ranks = jnp.sum(before * onehot, axis=2)
    retained = (flat_ids < EXPERTS) & (ranks < CAP)
    blocks = jnp.arange(n_blocks, dtype=jnp.int32)[:, None]
    source = blocks // GROUPS
    member = blocks % GROUPS
    overall = GROUPS * EXPERTS * SLOTS
    target = (member * EXPERTS + flat_ids) * SLOTS + source * CAP + ranks
    target = jnp.where(retained, target, overall).reshape(-1).astype(jnp.int32)
    routes = jnp.arange(TOK_DEV * TOPK, dtype=jnp.int32)[None, :]
    tokens = (blocks * TOK_DEV + routes // TOPK).reshape(-1).astype(jnp.int32)
    token_of = jnp.zeros((overall + 1,), jnp.int32).at[target].set(tokens)
    gate_of = jnp.zeros((overall + 1,), jnp.float32).at[target].set(gate_table.reshape(-1).astype(jnp.float32))
    return token_of[:overall], gate_of[:overall]


def section_weights(upstream, id_table, gate_table, inputs_section):
    token_of, gate_of = route_tables(id_table, gate_table)
    scaled = (jnp.take(upstream, token_of, axis=0).astype(jnp.float32) * gate_of[:, None]).astype(jnp.bfloat16)
    scaled = scaled.reshape(GROUPS, EXPERTS, SLOTS, D)
    accumulated = jnp.zeros((EXPERTS, D, HID), jnp.float32)
    for member in range(GROUPS):
        inputs_now = inputs_section[member].reshape(SLOTS, EXPERTS, HID).astype(jnp.float32)
        partial_value = jnp.einsum("esd,seh->edh", scaled[member].astype(jnp.float32), inputs_now)
        rounded = lax.optimization_barrier(partial_value.astype(jnp.bfloat16))
        accumulated = accumulated + rounded.astype(jnp.float32)
    result = accumulated.astype(jnp.bfloat16)
    return jnp.transpose(result, (1, 0, 2)).reshape(D, EXPERTS * HID)


def reference(section_grad, loss_grad, expert_ids, gate_values, down_inputs):
    results = []
    for section_index in range(SECTIONS):
        if section_index + 1 < SECTIONS:
            upstream = section_grad[section_index + 1]
        else:
            upstream = loss_grad
        results.append(section_weights(upstream, expert_ids[section_index], gate_values[section_index], down_inputs[section_index]))
    return jnp.stack(results, axis=0)
```

```python
import functools

import jax
import jax.numpy as jnp
from jax import lax
from jax.experimental import pallas as pl
from jax.experimental.pallas import tpu as pltpu
from jax.sharding import PartitionSpec as P

ROUTED = 256
SPLIT = 4
TILE = 16
LANES = 128
VMEM = pl.BlockSpec(memory_space=pltpu.VMEM)
ANY = pl.BlockSpec(memory_space=pl.ANY)


def each(count, body):
    if count <= 16:
        for i in range(count):
            body(i)
    else:
        lax.fori_loop(0, count, lambda i, c: (body(i), c)[1], 0)


def dot(a, b, contract):
    return lax.dot_general(a, b, ((contract[0], contract[1]), ((), ())), preferred_element_type=jnp.float32)


def chunk_starts(width, pack):
    size = -(-width // (pack * LANES)) * LANES
    return size, [min(c * size, width - size) for c in range(pack)]


def make_selector(ids, gates, expert, cap):
    tokens = ids.shape[1]
    found = ids == expert
    ones = jnp.ones((TILE, ids.shape[0]), jnp.float32)
    hit = jnp.sum(jnp.where(found, 1.0, 0.0), axis=0, keepdims=True)
    gate = jnp.sum(jnp.where(found, gates, 0.0), axis=0, keepdims=True)
    hit = jnp.broadcast_to(hit, (TILE, tokens))
    gate = jnp.broadcast_to(gate, (TILE, tokens))
    earlier = lax.broadcasted_iota(jnp.int32, (tokens, tokens), 0) < lax.broadcasted_iota(
        jnp.int32, (tokens, tokens), 1
    )
    before = jnp.where(earlier, 1.0, 0.0).astype(jnp.bfloat16)
    rank = dot(hit.astype(jnp.bfloat16), before, ((1,), (0,)))
    row = lax.broadcasted_iota(jnp.int32, (TILE, tokens), 0) % cap
    keep = (hit > 0.5) & (rank.astype(jnp.int32) == row)
    return jnp.where(keep, gate, 0.0).astype(jnp.bfloat16)


def gather_kernel(
    cap, ids_ref, gate_ref, grad_hbm, loss_hbm, inputs_ref,
    rows_ref, all_inputs_ref,
    sel_own, sel_in, grad_v, loss_v, out_a, out_b,
    load_sem, sel_sem, in_send, in_recv, send_a, send_b, recv_sem,
):
    pipes, cols, groups = lax.axis_size("pipe"), lax.axis_size("expert"), lax.axis_size("dp")
    p, e, g = lax.axis_index("pipe"), lax.axis_index("expert"), lax.axis_index("dp")
    experts = cols // SPLIT
    pack = TILE // cap
    width = grad_v.shape[1] // groups
    slots = inputs_ref.shape[0]
    size, starts = chunk_starts(width, pack)
    count = cols * groups
    me = e * groups + g
    last = p == pipes - 1
    slot = g * cols + e

    def place(pipe, col, group):
        return {"pipe": pipe, "expert": col, "dp": group}

    def load(src, dst, base, h):
        span = pl.ds(h * width, width)
        return pltpu.make_async_copy(src.at[:, span], dst.at[:, span], load_sem.at[base + h])

    def row_copy(pipe, i, source, sems):
        col, group = i // groups, i % groups
        return pltpu.make_async_remote_copy(
            src_ref=source.at[(col // SPLIT) * groups + group],
            dst_ref=rows_ref.at[slot],
            send_sem=sems.at[i],
            recv_sem=recv_sem.at[slot],
            device_id=place(pipe, col, group),
            device_id_type=pl.DeviceIdType.MESH,
        )

    def selector_copy():
        return pltpu.make_async_remote_copy(
            src_ref=sel_own, dst_ref=sel_in, send_sem=sel_sem.at[0], recv_sem=sel_sem.at[1],
            device_id=place(lax.rem(p + 1, pipes), e, g), device_id_type=pl.DeviceIdType.MESH,
        )

    def inputs_copy(group):
        return pltpu.make_async_remote_copy(
            src_ref=inputs_ref, dst_ref=all_inputs_ref.at[g],
            send_sem=in_send.at[group], recv_sem=in_recv.at[g],
            device_id=place(p, e, group), device_id_type=pl.DeviceIdType.MESH,
        )

    def other_group(k):
        return lax.rem(g + 1 + k, groups)

    def other_device(k):
        return lax.rem(me + 1 + k, count)

    @pl.when(last)
    def _():
        for h in range(groups):
            load(loss_hbm, loss_v, groups, h).start()

    @pl.when(p >= 1)
    def _():
        for h in range(groups):
            load(grad_hbm, grad_v, 0, h).start()

    barrier = pltpu.get_barrier_semaphore()

    def greet(pipe, col, group):
        pl.semaphore_signal(
            barrier, inc=1, device_id=place(pipe, col, group), device_id_type=pl.DeviceIdType.MESH
        )

    @pl.when(p >= 1)
    def _():
        greet(p - 1, e, g)

    for k in range(groups - 1):
        greet(p, e, other_group(k))

    @pl.when(jnp.logical_not(last))
    def _():
        each(count, lambda i: greet(p + 1, i // groups, i % groups))

    @pl.when(last)
    def _():
        def one(k):
            i = other_device(k)
            greet(p, i // groups, i % groups)
        each(count - 1, one)

    ids = ids_ref[...]
    gates = gate_ref[...].astype(jnp.float32)
    for x in range(experts):
        sel_own[x] = make_selector(ids, gates, x, cap)
    all_inputs_ref[g] = inputs_ref[...]

    targets = groups - 1 + jnp.where(p >= 1, count, 0) + jnp.where(last, count - 1, 1)
    pl.semaphore_wait(barrier, targets)

    @pl.when(jnp.logical_not(last))
    def _():
        selector_copy().start()

    for k in range(groups - 1):
        inputs_copy(other_group(k)).start()

    def pick(sel_ref, values, out, h):
        for x in range(experts):
            sel = sel_ref[x].astype(jnp.float32)
            chunk = lax.broadcasted_iota(jnp.int32, sel.shape, 0) // cap
            total = None
            for c in range(pack):
                part = jnp.where(chunk == c, sel, 0.0).astype(jnp.bfloat16)
                term = dot(part, values[:, pl.ds(h * width + starts[c], size)], ((1,), (0,)))
                total = term if total is None else total + term
            out[x * groups + h] = total.astype(jnp.bfloat16)

    @pl.when(last)
    def _():
        for h in range(groups):
            load(loss_hbm, loss_v, groups, h).wait()
            pick(sel_own, loss_v, out_b, h)
        rows_ref[slot] = out_b[(e // SPLIT) * groups + g]
        each(count - 1, lambda k: row_copy(p, other_device(k), out_b, send_b).start())

    @pl.when(p >= 1)
    def _():
        selector_copy().wait_recv()
        for h in range(groups):
            load(grad_hbm, grad_v, 0, h).wait()
            pick(sel_in, grad_v, out_a, h)
            each(cols, lambda k: row_copy(p - 1, k * groups + h, out_a, send_a).start())

    def arrived(i):
        return pltpu.make_async_remote_copy(
            src_ref=out_a.at[0], dst_ref=rows_ref.at[i], send_sem=send_a.at[0], recv_sem=recv_sem.at[i],
            device_id=place(p, e, g), device_id_type=pl.DeviceIdType.MESH,
        )

    @pl.when(jnp.logical_not(last))
    def _():
        each(count, lambda i: arrived(i).wait_recv())
        selector_copy().wait_send()

    @pl.when(last)
    def _():
        each(count - 1, lambda k: arrived(lax.rem(slot + 1 + k, count)).wait_recv())
        each(count - 1, lambda k: row_copy(p, other_device(k), out_b, send_b).wait_send())

    @pl.when(p >= 1)
    def _():
        each(count, lambda i: row_copy(p - 1, i, out_a, send_a).wait_send())

    for k in range(groups - 1):
        group = other_group(k)
        pltpu.make_async_remote_copy(
            src_ref=inputs_ref, dst_ref=all_inputs_ref.at[group],
            send_sem=in_send.at[group], recv_sem=in_recv.at[group],
            device_id=place(p, e, group), device_id_type=pl.DeviceIdType.MESH,
        ).wait()


def product_kernel(cap, starts, rows_ref, inputs_ref, out_ref):
    sources, tile, size = rows_ref.shape
    pack = tile // cap
    depth = sources * tile
    groups, slots, hidden = inputs_ref.shape
    inputs = inputs_ref[...].reshape(groups * slots, hidden)
    r = lax.broadcasted_iota(jnp.int32, (depth, groups * slots), 0)
    s = lax.broadcasted_iota(jnp.int32, (depth, groups * slots), 1)
    spread = jnp.where((r // tile == s // cap) & (r % cap == s % cap), 1.0, 0.0).astype(jnp.bfloat16)
    wide = dot(spread, inputs, ((1,), (0,)))
    chunk = (lax.broadcasted_iota(jnp.int32, wide.shape, 0) // cap) % pack
    weights = jnp.concatenate(
        [jnp.where(chunk == c, wide, 0.0).astype(jnp.bfloat16) for c in range(pack)], axis=1
    )
    for k in range(size // LANES):
        part = rows_ref[:, :, k * LANES:(k + 1) * LANES].reshape(depth, LANES)
        value = dot(part, weights, ((0,), (0,))).astype(out_ref.dtype)
        for c in range(pack):
            out_ref[starts[c] + k * LANES:starts[c] + (k + 1) * LANES, :] = value[:, c * hidden:(c + 1) * hidden]


def local(section_grad, loss_grad, expert_ids, gate_values, down_inputs):
    cols, groups = lax.axis_size("expert"), lax.axis_size("dp")
    experts = cols // SPLIT
    tokens, depth = section_grad.shape[1:]
    topk = expert_ids.shape[2]
    cap = tokens * topk // ROUTED
    pack = TILE // cap
    width = depth // groups
    size, starts = chunk_starts(width, pack)
    slots, hidden = down_inputs.shape[2:]
    count = cols * groups
    bf16 = jnp.bfloat16
    dma = pltpu.SemaphoreType.DMA
    rows, inputs = pl.pallas_call(
        functools.partial(gather_kernel, cap),
        out_shape=[
            jax.ShapeDtypeStruct((count, TILE, size), bf16),
            jax.ShapeDtypeStruct((groups, slots, hidden), bf16),
        ],
        in_specs=[VMEM, VMEM, ANY, ANY, VMEM],
        out_specs=[VMEM, VMEM],
        scratch_shapes=[
            pltpu.VMEM((experts, TILE, tokens), bf16),
            pltpu.VMEM((experts, TILE, tokens), bf16),
            pltpu.VMEM((tokens, depth), bf16),
            pltpu.VMEM((tokens, depth), bf16),
            pltpu.VMEM((experts * groups, TILE, size), bf16),
            pltpu.VMEM((experts * groups, TILE, size), bf16),
            dma((2 * groups,)),
            dma((2,)),
            dma((groups,)),
            dma((groups,)),
            dma((count,)),
            dma((count,)),
            dma((count,)),
        ],
        compiler_params=pltpu.CompilerParams(
            collective_id=0, has_side_effects=True, vmem_limit_bytes=32 << 20
        ),
    )(
        jnp.swapaxes(expert_ids[0], 0, 1),
        jnp.swapaxes(gate_values[0], 0, 1),
        section_grad[0],
        loss_grad,
        down_inputs[0, 0],
    )
    out = pl.pallas_call(
        functools.partial(product_kernel, cap, starts),
        out_shape=jax.ShapeDtypeStruct((width, hidden), bf16),
        in_specs=[VMEM, VMEM],
        out_specs=VMEM,
        compiler_params=pltpu.CompilerParams(vmem_limit_bytes=32 << 20),
    )(rows, inputs)
    return out[None]


def solution(mesh):
    in_specs = (
        P("pipe", ("expert", "dp"), None),
        P(("expert", "dp"), None),
        P("pipe", ("expert", "dp"), None),
        P("pipe", ("expert", "dp"), None),
        P("pipe", "dp", None, "expert"),
    )
    out_specs = P("pipe", "dp", "expert")
    return jax.shard_map(local, mesh=mesh, in_specs=in_specs, out_specs=out_specs, check_vma=False)
```

```python
import functools

import jax
import jax.numpy as jnp
from jax import lax
from jax.experimental import pallas as pl
from jax.experimental.pallas import tpu as pltpu
from jax.sharding import PartitionSpec as P

ROUTED = 256
SPLIT = 4
TILE = 16
LANES = 128
VMEM = pl.BlockSpec(memory_space=pltpu.VMEM)
HBM = pl.BlockSpec(memory_space=pltpu.HBM)


def each(count, body):
    if count <= 16:
        for i in range(count):
            body(i)
    else:
        lax.fori_loop(0, count, lambda i, c: (body(i), c)[1], 0)


def dot(a, b, contract):
    return lax.dot_general(a, b, ((contract[0], contract[1]), ((), ())), preferred_element_type=jnp.float32)


def chunk_starts(width, pack):
    size = -(-width // (pack * LANES)) * LANES
    return size, [min(c * size, width - size) for c in range(pack)]


def make_selector(ids, gates, expert, cap):
    tokens = ids.shape[1]
    found = ids == expert
    ones = jnp.ones((TILE, ids.shape[0]), jnp.float32)
    hit = jnp.sum(jnp.where(found, 1.0, 0.0), axis=0, keepdims=True)
    gate = jnp.sum(jnp.where(found, gates, 0.0), axis=0, keepdims=True)
    hit = jnp.broadcast_to(hit, (TILE, tokens))
    gate = jnp.broadcast_to(gate, (TILE, tokens))
    earlier = lax.broadcasted_iota(jnp.int32, (tokens, tokens), 0) < lax.broadcasted_iota(
        jnp.int32, (tokens, tokens), 1
    )
    before = jnp.where(earlier, 1.0, 0.0).astype(jnp.bfloat16)
    rank = dot(hit.astype(jnp.bfloat16), before, ((1,), (0,)))
    row = lax.broadcasted_iota(jnp.int32, (TILE, tokens), 0) % cap
    keep = (hit > 0.5) & (rank.astype(jnp.int32) == row)
    return jnp.where(keep, gate, 0.0).astype(jnp.bfloat16)


def gather_kernel(
    cap, ids_hbm, gate_hbm, grad_hbm, loss_hbm, inputs_hbm,
    rows_ref, all_inputs_ref,
    ids_ref, gate_ref, inputs_ref, sel_own, sel_in, grad_v, loss_v, out_a, out_b,
    small_sem, load_sem, sel_sem, in_send, in_recv, send_a, send_b, recv_sem,
):
    pipes, cols, groups = lax.axis_size("pipe"), lax.axis_size("expert"), lax.axis_size("dp")
    p, e, g = lax.axis_index("pipe"), lax.axis_index("expert"), lax.axis_index("dp")
    experts = cols // SPLIT
    pack = TILE // cap
    width = grad_v.shape[1] // groups
    slots = inputs_ref.shape[0]
    size, starts = chunk_starts(width, pack)
    count = cols * groups
    me = e * groups + g
    last = p == pipes - 1
    slot = g * cols + e

    def place(pipe, col, group):
        return {"pipe": pipe, "expert": col, "dp": group}

    def load(src, dst, base, h):
        span = pl.ds(h * width, width)
        return pltpu.make_async_copy(src.at[:, span], dst.at[:, span], load_sem.at[base + h])

    def row_copy(pipe, i, source, sems):
        col, group = i // groups, i % groups
        return pltpu.make_async_remote_copy(
            src_ref=source.at[(col // SPLIT) * groups + group],
            dst_ref=rows_ref.at[slot],
            send_sem=sems.at[i],
            recv_sem=recv_sem.at[slot],
            device_id=place(pipe, col, group),
            device_id_type=pl.DeviceIdType.MESH,
        )

    def selector_copy():
        return pltpu.make_async_remote_copy(
            src_ref=sel_own, dst_ref=sel_in, send_sem=sel_sem.at[0], recv_sem=sel_sem.at[1],
            device_id=place(lax.rem(p + 1, pipes), e, g), device_id_type=pl.DeviceIdType.MESH,
        )

    def inputs_copy(group):
        return pltpu.make_async_remote_copy(
            src_ref=inputs_ref, dst_ref=all_inputs_ref.at[g],
            send_sem=in_send.at[group], recv_sem=in_recv.at[g],
            device_id=place(p, e, group), device_id_type=pl.DeviceIdType.MESH,
        )

    def other_group(k):
        return lax.rem(g + 1 + k, groups)

    def other_device(k):
        return lax.rem(me + 1 + k, count)

    small = [
        pltpu.make_async_copy(src, dst, small_sem.at[i])
        for i, (src, dst) in enumerate(((ids_hbm, ids_ref), (gate_hbm, gate_ref), (inputs_hbm, inputs_ref)))
    ]
    for copy in small:
        copy.start()

    barrier = pltpu.get_barrier_semaphore()

    def greet(pipe, col, group):
        pl.semaphore_signal(
            barrier, inc=1, device_id=place(pipe, col, group), device_id_type=pl.DeviceIdType.MESH
        )

    @pl.when(p >= 1)
    def _():
        greet(p - 1, e, g)

    for k in range(groups - 1):
        greet(p, e, other_group(k))

    @pl.when(jnp.logical_not(last))
    def _():
        each(count, lambda i: greet(p + 1, i // groups, i % groups))

    @pl.when(last)
    def _():
        def one(k):
            i = other_device(k)
            greet(p, i // groups, i % groups)
        each(count - 1, one)

    @pl.when(last)
    def _():
        for h in range(groups):
            load(loss_hbm, loss_v, groups, h).start()

    @pl.when(p >= 1)
    def _():
        for h in range(groups):
            load(grad_hbm, grad_v, 0, h).start()

    for copy in small:
        copy.wait()
    ids = ids_ref[...]
    gates = gate_ref[...].astype(jnp.float32)
    for x in range(experts):
        sel_own[x] = make_selector(ids, gates, x, cap)
    all_inputs_ref[g] = inputs_ref[...]

    targets = groups - 1 + jnp.where(p >= 1, count, 0) + jnp.where(last, count - 1, 1)
    pl.semaphore_wait(barrier, targets)

    @pl.when(jnp.logical_not(last))
    def _():
        selector_copy().start()

    for k in range(groups - 1):
        inputs_copy(other_group(k)).start()

    def pick(sel_ref, values, out, h):
        for x in range(experts):
            sel = sel_ref[x].astype(jnp.float32)
            chunk = lax.broadcasted_iota(jnp.int32, sel.shape, 0) // cap
            total = None
            for c in range(pack):
                part = jnp.where(chunk == c, sel, 0.0).astype(jnp.bfloat16)
                term = dot(part, values[:, pl.ds(h * width + starts[c], size)], ((1,), (0,)))
                total = term if total is None else total + term
            out[x * groups + h] = total.astype(jnp.bfloat16)

    @pl.when(last)
    def _():
        for h in range(groups):
            load(loss_hbm, loss_v, groups, h).wait()
            pick(sel_own, loss_v, out_b, h)
        rows_ref[slot] = out_b[(e // SPLIT) * groups + g]
        each(count - 1, lambda k: row_copy(p, other_device(k), out_b, send_b).start())

    @pl.when(p >= 1)
    def _():
        selector_copy().wait_recv()
        for h in range(groups):
            load(grad_hbm, grad_v, 0, h).wait()
            pick(sel_in, grad_v, out_a, h)
            each(cols, lambda k: row_copy(p - 1, k * groups + h, out_a, send_a).start())

    def arrived(i):
        return pltpu.make_async_remote_copy(
            src_ref=out_a.at[0], dst_ref=rows_ref.at[i], send_sem=send_a.at[0], recv_sem=recv_sem.at[i],
            device_id=place(p, e, g), device_id_type=pl.DeviceIdType.MESH,
        )

    @pl.when(jnp.logical_not(last))
    def _():
        each(count, lambda i: arrived(i).wait_recv())
        selector_copy().wait_send()

    @pl.when(last)
    def _():
        each(count - 1, lambda k: arrived(lax.rem(slot + 1 + k, count)).wait_recv())
        each(count - 1, lambda k: row_copy(p, other_device(k), out_b, send_b).wait_send())

    @pl.when(p >= 1)
    def _():
        each(count, lambda i: row_copy(p - 1, i, out_a, send_a).wait_send())

    for k in range(groups - 1):
        group = other_group(k)
        pltpu.make_async_remote_copy(
            src_ref=inputs_ref, dst_ref=all_inputs_ref.at[group],
            send_sem=in_send.at[group], recv_sem=in_recv.at[group],
            device_id=place(p, e, group), device_id_type=pl.DeviceIdType.MESH,
        ).wait()


def product_kernel(cap, starts, rows_ref, inputs_ref, out_hbm, out_ref, sem):
    sources, tile, size = rows_ref.shape
    pack = tile // cap
    depth = sources * tile
    groups, slots, hidden = inputs_ref.shape
    inputs = inputs_ref[...].reshape(groups * slots, hidden)
    r = lax.broadcasted_iota(jnp.int32, (depth, groups * slots), 0)
    s = lax.broadcasted_iota(jnp.int32, (depth, groups * slots), 1)
    spread = jnp.where((r // tile == s // cap) & (r % cap == s % cap), 1.0, 0.0).astype(jnp.bfloat16)
    wide = dot(spread, inputs, ((1,), (0,)))
    chunk = (lax.broadcasted_iota(jnp.int32, wide.shape, 0) // cap) % pack
    weights = jnp.concatenate(
        [jnp.where(chunk == c, wide, 0.0).astype(jnp.bfloat16) for c in range(pack)], axis=1
    )
    apart = all(starts[c] == c * size for c in range(pack))
    copies = []

    def flush(first, rows):
        span = pl.ds(first, rows)
        copies.append(pltpu.make_async_copy(out_ref.at[span], out_hbm.at[span], sem.at[len(copies)]))
        copies[-1].start()

    for k in range(size // LANES):
        part = rows_ref[:, :, k * LANES:(k + 1) * LANES].reshape(depth, LANES)
        value = dot(part, weights, ((0,), (0,))).astype(out_ref.dtype)
        for c in range(pack):
            first = starts[c] + k * LANES
            out_ref[first:first + LANES, :] = value[:, c * hidden:(c + 1) * hidden]
            if apart:
                flush(first, LANES)
    if not apart:
        flush(0, out_ref.shape[0])
    for copy in copies:
        copy.wait()


def local(section_grad, loss_grad, expert_ids, gate_values, down_inputs):
    cols, groups = lax.axis_size("expert"), lax.axis_size("dp")
    experts = cols // SPLIT
    tokens, depth = section_grad.shape[1:]
    topk = expert_ids.shape[2]
    cap = tokens * topk // ROUTED
    pack = TILE // cap
    width = depth // groups
    size, starts = chunk_starts(width, pack)
    slots, hidden = down_inputs.shape[2:]
    count = cols * groups
    bf16 = jnp.bfloat16
    dma = pltpu.SemaphoreType.DMA
    rows, inputs = pl.pallas_call(
        functools.partial(gather_kernel, cap),
        out_shape=[
            jax.ShapeDtypeStruct((count, TILE, size), bf16),
            jax.ShapeDtypeStruct((groups, slots, hidden), bf16),
        ],
        in_specs=[HBM] * 5,
        out_specs=[VMEM, VMEM],
        scratch_shapes=[
            pltpu.VMEM((topk, tokens), expert_ids.dtype),
            pltpu.VMEM((topk, tokens), bf16),
            pltpu.VMEM((slots, hidden), bf16),
            pltpu.VMEM((experts, TILE, tokens), bf16),
            pltpu.VMEM((experts, TILE, tokens), bf16),
            pltpu.VMEM((tokens, depth), bf16),
            pltpu.VMEM((tokens, depth), bf16),
            pltpu.VMEM((experts * groups, TILE, size), bf16),
            pltpu.VMEM((experts * groups, TILE, size), bf16),
            dma((3,)),
            dma((2 * groups,)),
            dma((2,)),
            dma((groups,)),
            dma((groups,)),
            dma((count,)),
            dma((count,)),
            dma((count,)),
        ],
        compiler_params=pltpu.CompilerParams(
            collective_id=0, has_side_effects=True, vmem_limit_bytes=32 << 20
        ),
    )(
        jnp.swapaxes(expert_ids[0], 0, 1),
        jnp.swapaxes(gate_values[0], 0, 1),
        section_grad[0],
        loss_grad,
        down_inputs[0, 0],
    )
    out = pl.pallas_call(
        functools.partial(product_kernel, cap, starts),
        out_shape=jax.ShapeDtypeStruct((width, hidden), bf16),
        in_specs=[VMEM, VMEM],
        out_specs=HBM,
        scratch_shapes=[pltpu.VMEM((width, hidden), bf16), dma((pack * (size // LANES),))],
        compiler_params=pltpu.CompilerParams(vmem_limit_bytes=32 << 20),
    )(rows, inputs)
    return out[None]


def solution(mesh):
    in_specs = (
        P("pipe", ("expert", "dp"), None),
        P(("expert", "dp"), None),
        P("pipe", ("expert", "dp"), None),
        P("pipe", ("expert", "dp"), None),
        P("pipe", "dp", None, "expert"),
    )
    out_specs = P("pipe", "dp", "expert")
    return jax.shard_map(local, mesh=mesh, in_specs=in_specs, out_specs=out_specs, check_vma=False)
```

```python
import functools

import jax
import jax.numpy as jnp
from jax import lax
from jax.experimental import pallas as pl
from jax.experimental.pallas import tpu as pltpu
from jax.sharding import PartitionSpec as P

ROUTED = 256
SPLIT = 4
TILE = 16
LANES = 128
VMEM = pl.BlockSpec(memory_space=pltpu.VMEM)
HBM = pl.BlockSpec(memory_space=pltpu.HBM)


def each(count, body):
    if count <= 16:
        for i in range(count):
            body(i)
    else:
        lax.fori_loop(0, count, lambda i, c: (body(i), c)[1], 0)


def dot(a, b, contract):
    return lax.dot_general(a, b, ((contract[0], contract[1]), ((), ())), preferred_element_type=jnp.float32)


def chunk_starts(width, pack):
    size = -(-width // (pack * LANES)) * LANES
    return size, [min(c * size, width - size) for c in range(pack)]


def make_selector(ids, gates, expert, cap):
    tokens = ids.shape[1]
    found = ids == expert
    ones = jnp.ones((TILE, ids.shape[0]), jnp.float32)
    hit = jnp.sum(jnp.where(found, 1.0, 0.0), axis=0, keepdims=True)
    gate = jnp.sum(jnp.where(found, gates, 0.0), axis=0, keepdims=True)
    hit = jnp.broadcast_to(hit, (TILE, tokens))
    gate = jnp.broadcast_to(gate, (TILE, tokens))
    earlier = lax.broadcasted_iota(jnp.int32, (tokens, tokens), 0) < lax.broadcasted_iota(
        jnp.int32, (tokens, tokens), 1
    )
    before = jnp.where(earlier, 1.0, 0.0).astype(jnp.bfloat16)
    rank = dot(hit.astype(jnp.bfloat16), before, ((1,), (0,)))
    row = lax.broadcasted_iota(jnp.int32, (TILE, tokens), 0) % cap
    keep = (hit > 0.5) & (rank.astype(jnp.int32) == row)
    return jnp.where(keep, gate, 0.0).astype(jnp.bfloat16)


def gather_kernel(
    cap, ids_hbm, gate_hbm, grad_hbm, loss_hbm, inputs_hbm,
    rows_ref, all_inputs_ref,
    ids_ref, gate_ref, inputs_ref, sel_own, sel_in, grad_v, loss_v, out_a, out_b,
    small_sem, load_sem, sel_sem, in_send, in_recv, send_a, send_b, recv_sem,
):
    pipes, cols, groups = lax.axis_size("pipe"), lax.axis_size("expert"), lax.axis_size("dp")
    p, e, g = lax.axis_index("pipe"), lax.axis_index("expert"), lax.axis_index("dp")
    experts = cols // SPLIT
    pack = TILE // cap
    width = grad_v.shape[1] // groups
    slots = inputs_ref.shape[0]
    size, starts = chunk_starts(width, pack)
    count = cols * groups
    me = e * groups + g
    last = p == pipes - 1
    slot = g * cols + e

    def place(pipe, col, group):
        return {"pipe": pipe, "expert": col, "dp": group}

    def load(src, dst, base, h):
        span = pl.ds(h * width, width)
        return pltpu.make_async_copy(src.at[:, span], dst.at[:, span], load_sem.at[base + h])

    def row_copy(pipe, i, source, sems):
        col, group = i // groups, i % groups
        return pltpu.make_async_remote_copy(
            src_ref=source.at[(col // SPLIT) * groups + group],
            dst_ref=rows_ref.at[slot],
            send_sem=sems.at[i],
            recv_sem=recv_sem.at[slot],
            device_id=place(pipe, col, group),
            device_id_type=pl.DeviceIdType.MESH,
        )

    def selector_copy():
        return pltpu.make_async_remote_copy(
            src_ref=sel_own, dst_ref=sel_in, send_sem=sel_sem.at[0], recv_sem=sel_sem.at[1],
            device_id=place(lax.rem(p + 1, pipes), e, g), device_id_type=pl.DeviceIdType.MESH,
        )

    def inputs_copy(group):
        return pltpu.make_async_remote_copy(
            src_ref=inputs_ref, dst_ref=all_inputs_ref.at[g],
            send_sem=in_send.at[group], recv_sem=in_recv.at[g],
            device_id=place(p, e, group), device_id_type=pl.DeviceIdType.MESH,
        )

    def other_group(k):
        return lax.rem(g + 1 + k, groups)

    def other_device(k):
        return lax.rem(me + 1 + k, count)

    small = [
        pltpu.make_async_copy(src, dst, small_sem.at[i])
        for i, (src, dst) in enumerate(((ids_hbm, ids_ref), (gate_hbm, gate_ref), (inputs_hbm, inputs_ref)))
    ]
    for copy in small:
        copy.start()

    barrier = pltpu.get_barrier_semaphore()

    def greet(pipe, col, group):
        pl.semaphore_signal(
            barrier, inc=1, device_id=place(pipe, col, group), device_id_type=pl.DeviceIdType.MESH
        )

    @pl.when(p >= 1)
    def _():
        greet(p - 1, e, g)

    for k in range(groups - 1):
        greet(p, e, other_group(k))

    @pl.when(jnp.logical_not(last))
    def _():
        each(count, lambda i: greet(p + 1, i // groups, i % groups))

    @pl.when(last)
    def _():
        def one(k):
            i = other_device(k)
            greet(p, i // groups, i % groups)
        each(count - 1, one)

    @pl.when(last)
    def _():
        for h in range(groups):
            load(loss_hbm, loss_v, groups, h).start()

    @pl.when(p >= 1)
    def _():
        for h in range(groups):
            load(grad_hbm, grad_v, 0, h).start()

    for copy in small:
        copy.wait()
    ids = ids_ref[...]
    gates = gate_ref[...].astype(jnp.float32)
    for x in range(experts):
        sel_own[x] = make_selector(ids, gates, x, cap)
    all_inputs_ref[g] = inputs_ref[...]

    targets = groups - 1 + jnp.where(p >= 1, count, 0) + jnp.where(last, count - 1, 1)
    pl.semaphore_wait(barrier, targets)

    @pl.when(jnp.logical_not(last))
    def _():
        selector_copy().start()

    for k in range(groups - 1):
        inputs_copy(other_group(k)).start()

    def pick(sel_ref, values, out, h):
        for x in range(experts):
            sel = sel_ref[x].astype(jnp.float32)
            chunk = lax.broadcasted_iota(jnp.int32, sel.shape, 0) // cap
            total = None
            for c in range(pack):
                part = jnp.where(chunk == c, sel, 0.0).astype(jnp.bfloat16)
                term = dot(part, values[:, pl.ds(h * width + starts[c], size)], ((1,), (0,)))
                total = term if total is None else total + term
            out[x * groups + h] = total.astype(jnp.bfloat16)

    @pl.when(last)
    def _():
        for h in range(groups):
            load(loss_hbm, loss_v, groups, h).wait()
            pick(sel_own, loss_v, out_b, h)
        rows_ref[slot] = out_b[(e // SPLIT) * groups + g]
        each(count - 1, lambda k: row_copy(p, other_device(k), out_b, send_b).start())

    @pl.when(p >= 1)
    def _():
        selector_copy().wait_recv()
        for h in range(groups):
            load(grad_hbm, grad_v, 0, h).wait()
            pick(sel_in, grad_v, out_a, h)
            each(cols, lambda k: row_copy(p - 1, k * groups + h, out_a, send_a).start())

    def arrived(i):
        return pltpu.make_async_remote_copy(
            src_ref=out_a.at[0], dst_ref=rows_ref.at[i], send_sem=send_a.at[0], recv_sem=recv_sem.at[i],
            device_id=place(p, e, g), device_id_type=pl.DeviceIdType.MESH,
        )

    @pl.when(jnp.logical_not(last))
    def _():
        each(count, lambda i: arrived(i).wait_recv())
        selector_copy().wait_send()

    @pl.when(last)
    def _():
        each(count - 1, lambda k: arrived(lax.rem(slot + 1 + k, count)).wait_recv())
        each(count - 1, lambda k: row_copy(p, other_device(k), out_b, send_b).wait_send())

    @pl.when(p >= 1)
    def _():
        each(count, lambda i: row_copy(p - 1, i, out_a, send_a).wait_send())

    for k in range(groups - 1):
        group = other_group(k)
        pltpu.make_async_remote_copy(
            src_ref=inputs_ref, dst_ref=all_inputs_ref.at[group],
            send_sem=in_send.at[group], recv_sem=in_recv.at[group],
            device_id=place(p, e, group), device_id_type=pl.DeviceIdType.MESH,
        ).wait()


def product_kernel(cap, starts, rows_ref, inputs_ref, out_hbm, out_ref, sem):
    sources, tile, size = rows_ref.shape
    pack = tile // cap
    depth = sources * tile
    groups, slots, hidden = inputs_ref.shape
    inputs = inputs_ref[...].reshape(groups * slots, hidden)
    r = lax.broadcasted_iota(jnp.int32, (depth, groups * slots), 0)
    s = lax.broadcasted_iota(jnp.int32, (depth, groups * slots), 1)
    spread = jnp.where((r // tile == s // cap) & (r % cap == s % cap), 1.0, 0.0).astype(jnp.bfloat16)
    wide = dot(spread, inputs, ((1,), (0,)))
    chunk = (lax.broadcasted_iota(jnp.int32, wide.shape, 0) // cap) % pack
    weights = jnp.concatenate(
        [jnp.where(chunk == c, wide, 0.0).astype(jnp.bfloat16) for c in range(pack)], axis=1
    )
    apart = all(starts[c] == c * size for c in range(pack))
    copies = []

    def flush(first, rows):
        span = pl.ds(first, rows)
        copies.append(pltpu.make_async_copy(out_ref.at[span], out_hbm.at[span], sem.at[len(copies)]))
        copies[-1].start()

    for k in range(size // LANES):
        part = rows_ref[:, :, k * LANES:(k + 1) * LANES].reshape(depth, LANES)
        value = dot(part, weights, ((0,), (0,))).astype(out_ref.dtype)
        for c in range(pack):
            first = starts[c] + k * LANES
            out_ref[first:first + LANES, :] = value[:, c * hidden:(c + 1) * hidden]
            if apart:
                flush(first, LANES)
    if not apart:
        flush(0, out_ref.shape[0])
    for copy in copies:
        copy.wait()


def local(section_grad, loss_grad, expert_ids, gate_values, down_inputs):
    cols, groups = lax.axis_size("expert"), lax.axis_size("dp")
    experts = cols // SPLIT
    tokens, depth = section_grad.shape[1:]
    topk = expert_ids.shape[2]
    cap = tokens * topk // ROUTED
    pack = TILE // cap
    width = depth // groups
    size, starts = chunk_starts(width, pack)
    slots, hidden = down_inputs.shape[2:]
    count = cols * groups
    bf16 = jnp.bfloat16
    dma = pltpu.SemaphoreType.DMA
    rows, inputs = pl.pallas_call(
        functools.partial(gather_kernel, cap),
        out_shape=[
            jax.ShapeDtypeStruct((count, TILE, size), bf16),
            jax.ShapeDtypeStruct((groups, slots, hidden), bf16),
        ],
        in_specs=[HBM] * 5,
        out_specs=[VMEM, VMEM],
        scratch_shapes=[
            pltpu.VMEM((topk, tokens), expert_ids.dtype),
            pltpu.VMEM((topk, tokens), bf16),
            pltpu.VMEM((slots, hidden), bf16),
            pltpu.VMEM((experts, TILE, tokens), bf16),
            pltpu.VMEM((experts, TILE, tokens), bf16),
            pltpu.VMEM((tokens, depth), bf16),
            pltpu.VMEM((tokens, depth), bf16),
            pltpu.VMEM((experts * groups, TILE, size), bf16),
            pltpu.VMEM((experts * groups, TILE, size), bf16),
            dma((3,)),
            dma((2 * groups,)),
            dma((2,)),
            dma((groups,)),
            dma((groups,)),
            dma((count,)),
            dma((count,)),
            dma((count,)),
        ],
        compiler_params=pltpu.CompilerParams(
            collective_id=0, has_side_effects=True, vmem_limit_bytes=32 << 20
        ),
    )(
        *(
            pltpu.with_memory_space_constraint(x, pltpu.HBM)
            for x in (
                jnp.swapaxes(expert_ids[0], 0, 1),
                jnp.swapaxes(gate_values[0], 0, 1),
                section_grad[0],
                loss_grad,
                down_inputs[0, 0],
            )
        )
    )
    out = pl.pallas_call(
        functools.partial(product_kernel, cap, starts),
        out_shape=jax.ShapeDtypeStruct((width, hidden), bf16),
        in_specs=[VMEM, VMEM],
        out_specs=HBM,
        scratch_shapes=[pltpu.VMEM((width, hidden), bf16), dma((pack * (size // LANES),))],
        compiler_params=pltpu.CompilerParams(vmem_limit_bytes=32 << 20),
    )(rows, inputs)
    return out[None]


def solution(mesh):
    in_specs = (
        P("pipe", ("expert", "dp"), None),
        P(("expert", "dp"), None),
        P("pipe", ("expert", "dp"), None),
        P("pipe", ("expert", "dp"), None),
        P("pipe", "dp", None, "expert"),
    )
    out_specs = P("pipe", "dp", "expert")
    return jax.shard_map(local, mesh=mesh, in_specs=in_specs, out_specs=out_specs, check_vma=False)
```

```python
import functools

import jax
import jax.numpy as jnp
from jax import lax
from jax.experimental import pallas as pl
from jax.experimental.pallas import tpu as pltpu
from jax.sharding import PartitionSpec as P

ROUTED = 256
SPLIT = 4
TILE = 16
LANES = 128
VMEM = pl.BlockSpec(memory_space=pltpu.VMEM)
HBM = pl.BlockSpec(memory_space=pltpu.HBM)


def each(count, body):
    if count <= 16:
        for i in range(count):
            body(i)
    else:
        lax.fori_loop(0, count, lambda i, c: (body(i), c)[1], 0)


def dot(a, b, contract):
    return lax.dot_general(a, b, ((contract[0], contract[1]), ((), ())), preferred_element_type=jnp.float32)


def chunk_starts(width, pack):
    size = -(-width // (pack * LANES)) * LANES
    return size, [min(c * size, width - size) for c in range(pack)]


def make_selector(ids, gates, expert, cap):
    tokens = ids.shape[1]
    found = ids == expert
    ones = jnp.ones((TILE, ids.shape[0]), jnp.float32)
    hit = jnp.sum(jnp.where(found, 1.0, 0.0), axis=0, keepdims=True)
    gate = jnp.sum(jnp.where(found, gates, 0.0), axis=0, keepdims=True)
    hit = jnp.broadcast_to(hit, (TILE, tokens))
    gate = jnp.broadcast_to(gate, (TILE, tokens))
    earlier = lax.broadcasted_iota(jnp.int32, (tokens, tokens), 0) < lax.broadcasted_iota(
        jnp.int32, (tokens, tokens), 1
    )
    before = jnp.where(earlier, 1.0, 0.0).astype(jnp.bfloat16)
    rank = dot(hit.astype(jnp.bfloat16), before, ((1,), (0,)))
    row = lax.broadcasted_iota(jnp.int32, (TILE, tokens), 0) % cap
    keep = (hit > 0.5) & (rank.astype(jnp.int32) == row)
    return jnp.where(keep, gate, 0.0).astype(jnp.bfloat16)


def gather_kernel(
    cap, ids_hbm, gate_hbm, grad_hbm, loss_hbm, inputs_hbm,
    rows_ref, all_inputs_ref,
    ids_ref, gate_ref, inputs_ref, sel_own, sel_in, grad_v, out,
    small_sem, load_sem, sel_sem, in_send, in_recv, send_sem, recv_sem,
):
    pipes, cols, groups = lax.axis_size("pipe"), lax.axis_size("expert"), lax.axis_size("dp")
    p, e, g = lax.axis_index("pipe"), lax.axis_index("expert"), lax.axis_index("dp")
    experts = cols // SPLIT
    pack = TILE // cap
    width = grad_v.shape[1] // groups
    slots = inputs_ref.shape[0]
    size, starts = chunk_starts(width, pack)
    count = cols * groups
    me = e * groups + g
    after, before = lax.rem(p + 1, pipes), lax.rem(p + pipes - 1, pipes)
    slot = g * cols + e

    def place(pipe, col, group):
        return {"pipe": pipe, "expert": col, "dp": group}

    def load(src, h):
        span = pl.ds(h * width, width)
        return pltpu.make_async_copy(src.at[:, span], grad_v.at[:, span], load_sem.at[h])

    def row_copy(i):
        col, group = i // groups, i % groups
        return pltpu.make_async_remote_copy(
            src_ref=out.at[(col // SPLIT) * groups + group],
            dst_ref=rows_ref.at[slot],
            send_sem=send_sem.at[i],
            recv_sem=recv_sem.at[slot],
            device_id=place(before, col, group),
            device_id_type=pl.DeviceIdType.MESH,
        )

    def selector_copy():
        return pltpu.make_async_remote_copy(
            src_ref=sel_own, dst_ref=sel_in, send_sem=sel_sem.at[0], recv_sem=sel_sem.at[1],
            device_id=place(after, e, g), device_id_type=pl.DeviceIdType.MESH,
        )

    def inputs_copy(group):
        return pltpu.make_async_remote_copy(
            src_ref=inputs_ref, dst_ref=all_inputs_ref.at[g],
            send_sem=in_send.at[group], recv_sem=in_recv.at[g],
            device_id=place(p, e, group), device_id_type=pl.DeviceIdType.MESH,
        )

    def other_group(k):
        return lax.rem(g + 1 + k, groups)

    small = [
        pltpu.make_async_copy(src, dst, small_sem.at[i])
        for i, (src, dst) in enumerate(((ids_hbm, ids_ref), (gate_hbm, gate_ref), (inputs_hbm, inputs_ref)))
    ]
    for copy in small:
        copy.start()

    barrier = pltpu.get_barrier_semaphore()

    def greet(pipe, col, group):
        pl.semaphore_signal(
            barrier, inc=1, device_id=place(pipe, col, group), device_id_type=pl.DeviceIdType.MESH
        )

    greet(before, e, g)
    for k in range(groups - 1):
        greet(p, e, other_group(k))
    each(count, lambda i: greet(after, i // groups, i % groups))

    @pl.when(p == 0)
    def _():
        for h in range(groups):
            load(loss_hbm, h).start()

    @pl.when(p >= 1)
    def _():
        for h in range(groups):
            load(grad_hbm, h).start()

    for copy in small:
        copy.wait()
    ids = ids_ref[...]
    gates = gate_ref[...].astype(jnp.float32)
    for x in range(experts):
        sel_own[x] = make_selector(ids, gates, x, cap)
    all_inputs_ref[g] = inputs_ref[...]

    pl.semaphore_wait(barrier, count + groups)
    selector_copy().start()
    for k in range(groups - 1):
        inputs_copy(other_group(k)).start()

    def pick(h):
        for x in range(experts):
            sel = sel_in[x].astype(jnp.float32)
            chunk = lax.broadcasted_iota(jnp.int32, sel.shape, 0) // cap
            total = None
            for c in range(pack):
                part = jnp.where(chunk == c, sel, 0.0).astype(jnp.bfloat16)
                term = dot(part, grad_v[:, pl.ds(h * width + starts[c], size)], ((1,), (0,)))
                total = term if total is None else total + term
            out[x * groups + h] = total.astype(jnp.bfloat16)

    selector_copy().wait_recv()
    for h in range(groups):
        load(grad_hbm, h).wait()
        pick(h)
        each(cols, lambda k: row_copy(lax.rem(e + 1 + k, cols) * groups + h).start())

    def arrived(i):
        return pltpu.make_async_remote_copy(
            src_ref=out.at[0], dst_ref=rows_ref.at[i], send_sem=send_sem.at[0], recv_sem=recv_sem.at[i],
            device_id=place(p, e, g), device_id_type=pl.DeviceIdType.MESH,
        )

    each(count, lambda i: arrived(i).wait_recv())
    selector_copy().wait_send()
    each(count, lambda i: row_copy(i).wait_send())
    for k in range(groups - 1):
        group = other_group(k)
        pltpu.make_async_remote_copy(
            src_ref=inputs_ref, dst_ref=all_inputs_ref.at[group],
            send_sem=in_send.at[group], recv_sem=in_recv.at[group],
            device_id=place(p, e, group), device_id_type=pl.DeviceIdType.MESH,
        ).wait()


def product_kernel(cap, starts, rows_ref, inputs_ref, out_hbm, out_ref, sem):
    sources, tile, size = rows_ref.shape
    pack = tile // cap
    depth = sources * tile
    groups, slots, hidden = inputs_ref.shape
    inputs = inputs_ref[...].reshape(groups * slots, hidden)
    r = lax.broadcasted_iota(jnp.int32, (depth, groups * slots), 0)
    s = lax.broadcasted_iota(jnp.int32, (depth, groups * slots), 1)
    spread = jnp.where((r // tile == s // cap) & (r % cap == s % cap), 1.0, 0.0).astype(jnp.bfloat16)
    wide = dot(spread, inputs, ((1,), (0,)))
    chunk = (lax.broadcasted_iota(jnp.int32, wide.shape, 0) // cap) % pack
    weights = jnp.concatenate(
        [jnp.where(chunk == c, wide, 0.0).astype(jnp.bfloat16) for c in range(pack)], axis=1
    )
    apart = all(starts[c] == c * size for c in range(pack))
    copies = []

    def flush(first, rows):
        span = pl.ds(first, rows)
        copies.append(pltpu.make_async_copy(out_ref.at[span], out_hbm.at[span], sem.at[len(copies)]))
        copies[-1].start()

    for k in range(size // LANES):
        part = rows_ref[:, :, k * LANES:(k + 1) * LANES].reshape(depth, LANES)
        value = dot(part, weights, ((0,), (0,))).astype(out_ref.dtype)
        for c in range(pack):
            first = starts[c] + k * LANES
            out_ref[first:first + LANES, :] = value[:, c * hidden:(c + 1) * hidden]
            if apart:
                flush(first, LANES)
    if not apart:
        flush(0, out_ref.shape[0])
    for copy in copies:
        copy.wait()


def local(section_grad, loss_grad, expert_ids, gate_values, down_inputs):
    cols, groups = lax.axis_size("expert"), lax.axis_size("dp")
    experts = cols // SPLIT
    tokens, depth = section_grad.shape[1:]
    topk = expert_ids.shape[2]
    cap = tokens * topk // ROUTED
    pack = TILE // cap
    width = depth // groups
    size, starts = chunk_starts(width, pack)
    slots, hidden = down_inputs.shape[2:]
    count = cols * groups
    bf16 = jnp.bfloat16
    dma = pltpu.SemaphoreType.DMA
    rows, inputs = pl.pallas_call(
        functools.partial(gather_kernel, cap),
        out_shape=[
            jax.ShapeDtypeStruct((count, TILE, size), bf16),
            jax.ShapeDtypeStruct((groups, slots, hidden), bf16),
        ],
        in_specs=[HBM] * 5,
        out_specs=[VMEM, VMEM],
        scratch_shapes=[
            pltpu.VMEM((topk, tokens), expert_ids.dtype),
            pltpu.VMEM((topk, tokens), bf16),
            pltpu.VMEM((slots, hidden), bf16),
            pltpu.VMEM((experts, TILE, tokens), bf16),
            pltpu.VMEM((experts, TILE, tokens), bf16),
            pltpu.VMEM((tokens, depth), bf16),
            pltpu.VMEM((experts * groups, TILE, size), bf16),
            dma((3,)),
            dma((groups,)),
            dma((2,)),
            dma((groups,)),
            dma((groups,)),
            dma((count,)),
            dma((count,)),
        ],
        compiler_params=pltpu.CompilerParams(
            collective_id=0, has_side_effects=True, vmem_limit_bytes=32 << 20
        ),
    )(
        *(
            pltpu.with_memory_space_constraint(x, pltpu.HBM)
            for x in (
                jnp.swapaxes(expert_ids[0], 0, 1),
                jnp.swapaxes(gate_values[0], 0, 1),
                section_grad[0],
                loss_grad,
                down_inputs[0, 0],
            )
        )
    )
    out = pl.pallas_call(
        functools.partial(product_kernel, cap, starts),
        out_shape=jax.ShapeDtypeStruct((width, hidden), bf16),
        in_specs=[VMEM, VMEM],
        out_specs=HBM,
        scratch_shapes=[pltpu.VMEM((width, hidden), bf16), dma((pack * (size // LANES),))],
        compiler_params=pltpu.CompilerParams(vmem_limit_bytes=32 << 20),
    )(rows, inputs)
    return out[None]


def solution(mesh):
    in_specs = (
        P("pipe", ("expert", "dp"), None),
        P(("expert", "dp"), None),
        P("pipe", ("expert", "dp"), None),
        P("pipe", ("expert", "dp"), None),
        P("pipe", "dp", None, "expert"),
    )
    out_specs = P("pipe", "dp", "expert")
    return jax.shard_map(local, mesh=mesh, in_specs=in_specs, out_specs=out_specs, check_vma=False)
```

```python
import functools

import jax
import jax.numpy as jnp
from jax import lax
from jax.experimental import pallas as pl
from jax.experimental.pallas import tpu as pltpu
from jax.sharding import PartitionSpec as P

ROUTED = 256
SPLIT = 4
TILE = 16
LANES = 128
VMEM = pl.BlockSpec(memory_space=pltpu.VMEM)
HBM = pl.BlockSpec(memory_space=pltpu.HBM)


def each(count, body):
    if count <= 16:
        for i in range(count):
            body(i)
    else:
        lax.fori_loop(0, count, lambda i, c: (body(i), c)[1], 0)


def dot(a, b, contract):
    return lax.dot_general(a, b, ((contract[0], contract[1]), ((), ())), preferred_element_type=jnp.float32)


def chunk_starts(width, pack):
    size = -(-width // (pack * LANES)) * LANES
    return size, [min(c * size, width - size) for c in range(pack)]


def make_selector(ids, gates, expert, cap):
    tokens = ids.shape[1]
    found = ids == expert
    ones = jnp.ones((TILE, ids.shape[0]), jnp.float32)
    hit = jnp.sum(jnp.where(found, 1.0, 0.0), axis=0, keepdims=True)
    gate = jnp.sum(jnp.where(found, gates, 0.0), axis=0, keepdims=True)
    hit = jnp.broadcast_to(hit, (TILE, tokens))
    gate = jnp.broadcast_to(gate, (TILE, tokens))
    earlier = lax.broadcasted_iota(jnp.int32, (tokens, tokens), 0) < lax.broadcasted_iota(
        jnp.int32, (tokens, tokens), 1
    )
    before = jnp.where(earlier, 1.0, 0.0).astype(jnp.bfloat16)
    rank = dot(hit.astype(jnp.bfloat16), before, ((1,), (0,)))
    row = lax.broadcasted_iota(jnp.int32, (TILE, tokens), 0) % cap
    keep = (hit > 0.5) & (rank.astype(jnp.int32) == row)
    return jnp.where(keep, gate, 0.0).astype(jnp.bfloat16)


def gather_kernel(
    cap, ids_hbm, gate_hbm, grad_hbm, loss_hbm, inputs_hbm,
    rows_ref, weights_ref,
    all_inputs_ref, ids_ref, gate_ref, inputs_ref, sel_own, sel_in, grad_v, out,
    small_sem, load_sem, sel_sem, in_send, in_recv, send_sem, recv_sem,
):
    pipes, cols, groups = lax.axis_size("pipe"), lax.axis_size("expert"), lax.axis_size("dp")
    p, e, g = lax.axis_index("pipe"), lax.axis_index("expert"), lax.axis_index("dp")
    experts = cols // SPLIT
    pack = TILE // cap
    width = grad_v.shape[1] // groups
    slots = inputs_ref.shape[0]
    size, starts = chunk_starts(width, pack)
    count = cols * groups
    me = e * groups + g
    after, before = lax.rem(p + 1, pipes), lax.rem(p + pipes - 1, pipes)
    slot = g * cols + e

    def place(pipe, col, group):
        return {"pipe": pipe, "expert": col, "dp": group}

    def load(src, h):
        span = pl.ds(h * width, width)
        return pltpu.make_async_copy(src.at[:, span], grad_v.at[:, span], load_sem.at[h])

    def row_copy(i):
        col, group = i // groups, i % groups
        return pltpu.make_async_remote_copy(
            src_ref=out.at[(col // SPLIT) * groups + group],
            dst_ref=rows_ref.at[slot],
            send_sem=send_sem.at[i],
            recv_sem=recv_sem.at[slot],
            device_id=place(before, col, group),
            device_id_type=pl.DeviceIdType.MESH,
        )

    def selector_copy():
        return pltpu.make_async_remote_copy(
            src_ref=sel_own, dst_ref=sel_in, send_sem=sel_sem.at[0], recv_sem=sel_sem.at[1],
            device_id=place(after, e, g), device_id_type=pl.DeviceIdType.MESH,
        )

    def inputs_copy(group):
        return pltpu.make_async_remote_copy(
            src_ref=inputs_ref, dst_ref=all_inputs_ref.at[g],
            send_sem=in_send.at[group], recv_sem=in_recv.at[g],
            device_id=place(p, e, group), device_id_type=pl.DeviceIdType.MESH,
        )

    def other_group(k):
        return lax.rem(g + 1 + k, groups)

    small = [
        pltpu.make_async_copy(src, dst, small_sem.at[i])
        for i, (src, dst) in enumerate(((ids_hbm, ids_ref), (gate_hbm, gate_ref), (inputs_hbm, inputs_ref)))
    ]
    for copy in small:
        copy.start()

    barrier = pltpu.get_barrier_semaphore()

    def greet(pipe, col, group):
        pl.semaphore_signal(
            barrier, inc=1, device_id=place(pipe, col, group), device_id_type=pl.DeviceIdType.MESH
        )

    greet(before, e, g)
    for k in range(groups - 1):
        greet(p, e, other_group(k))
    each(count, lambda i: greet(after, i // groups, i % groups))

    @pl.when(p == 0)
    def _():
        for h in range(groups):
            load(loss_hbm, h).start()

    @pl.when(p >= 1)
    def _():
        for h in range(groups):
            load(grad_hbm, h).start()

    for copy in small:
        copy.wait()
    ids = ids_ref[...]
    gates = gate_ref[...].astype(jnp.float32)
    for x in range(experts):
        sel_own[x] = make_selector(ids, gates, x, cap)
    all_inputs_ref[g] = inputs_ref[...]

    pl.semaphore_wait(barrier, count + groups)
    selector_copy().start()
    for k in range(groups - 1):
        inputs_copy(other_group(k)).start()

    def pick(h):
        for x in range(experts):
            sel = sel_in[x].astype(jnp.float32)
            chunk = lax.broadcasted_iota(jnp.int32, sel.shape, 0) // cap
            total = None
            for c in range(pack):
                part = jnp.where(chunk == c, sel, 0.0).astype(jnp.bfloat16)
                term = dot(part, grad_v[:, pl.ds(h * width + starts[c], size)], ((1,), (0,)))
                total = term if total is None else total + term
            out[x * groups + h] = total.astype(jnp.bfloat16)

    selector_copy().wait_recv()
    for h in range(groups):
        load(grad_hbm, h).wait()
        pick(h)
        each(cols, lambda k: row_copy(lax.rem(e + 1 + k, cols) * groups + h).start())

    for k in range(groups - 1):
        group = other_group(k)
        pltpu.make_async_remote_copy(
            src_ref=inputs_ref, dst_ref=all_inputs_ref.at[group],
            send_sem=in_send.at[group], recv_sem=in_recv.at[group],
            device_id=place(p, e, group), device_id_type=pl.DeviceIdType.MESH,
        ).wait()
    weights_ref[...] = spread_inputs(all_inputs_ref[...], cap, count * TILE)

    def arrived(i):
        return pltpu.make_async_remote_copy(
            src_ref=out.at[0], dst_ref=rows_ref.at[i], send_sem=send_sem.at[0], recv_sem=recv_sem.at[i],
            device_id=place(p, e, g), device_id_type=pl.DeviceIdType.MESH,
        )

    each(count, lambda i: arrived(i).wait_recv())
    selector_copy().wait_send()
    each(count, lambda i: row_copy(i).wait_send())


def spread_inputs(inputs, cap, depth):
    groups, slots, hidden = inputs.shape
    inputs = inputs.reshape(groups * slots, hidden)
    r = lax.broadcasted_iota(jnp.int32, (depth, groups * slots), 0)
    s = lax.broadcasted_iota(jnp.int32, (depth, groups * slots), 1)
    spread = jnp.where((r // TILE == s // cap) & (r % cap == s % cap), 1.0, 0.0).astype(jnp.bfloat16)
    wide = dot(spread, inputs, ((1,), (0,)))
    chunk = (lax.broadcasted_iota(jnp.int32, wide.shape, 0) // cap) % (TILE // cap)
    return jnp.concatenate(
        [jnp.where(chunk == c, wide, 0.0).astype(jnp.bfloat16) for c in range(TILE // cap)], axis=1
    )


def product_kernel(starts, rows_ref, weights_ref, out_hbm, out_ref, sem):
    sources, tile, size = rows_ref.shape
    pack = len(starts)
    depth = sources * tile
    hidden = out_ref.shape[1]
    weights = weights_ref[...]
    apart = all(starts[c] == c * size for c in range(pack))
    copies = []

    def flush(first, rows):
        span = pl.ds(first, rows)
        copies.append(pltpu.make_async_copy(out_ref.at[span], out_hbm.at[span], sem.at[len(copies)]))
        copies[-1].start()

    for k in range(size // LANES):
        part = rows_ref[:, :, k * LANES:(k + 1) * LANES].reshape(depth, LANES)
        value = dot(part, weights, ((0,), (0,))).astype(out_ref.dtype)
        for c in range(pack):
            first = starts[c] + k * LANES
            out_ref[first:first + LANES, :] = value[:, c * hidden:(c + 1) * hidden]
            if apart:
                flush(first, LANES)
    if not apart:
        flush(0, out_ref.shape[0])
    for copy in copies:
        copy.wait()


def local(section_grad, loss_grad, expert_ids, gate_values, down_inputs):
    cols, groups = lax.axis_size("expert"), lax.axis_size("dp")
    experts = cols // SPLIT
    tokens, depth = section_grad.shape[1:]
    topk = expert_ids.shape[2]
    cap = tokens * topk // ROUTED
    pack = TILE // cap
    width = depth // groups
    size, starts = chunk_starts(width, pack)
    slots, hidden = down_inputs.shape[2:]
    count = cols * groups
    bf16 = jnp.bfloat16
    dma = pltpu.SemaphoreType.DMA
    rows, weights = pl.pallas_call(
        functools.partial(gather_kernel, cap),
        out_shape=[
            jax.ShapeDtypeStruct((count, TILE, size), bf16),
            jax.ShapeDtypeStruct((count * TILE, pack * hidden), bf16),
        ],
        in_specs=[HBM] * 5,
        out_specs=[VMEM, VMEM],
        scratch_shapes=[
            pltpu.VMEM((groups, slots, hidden), bf16),
            pltpu.VMEM((topk, tokens), expert_ids.dtype),
            pltpu.VMEM((topk, tokens), bf16),
            pltpu.VMEM((slots, hidden), bf16),
            pltpu.VMEM((experts, TILE, tokens), bf16),
            pltpu.VMEM((experts, TILE, tokens), bf16),
            pltpu.VMEM((tokens, depth), bf16),
            pltpu.VMEM((experts * groups, TILE, size), bf16),
            dma((3,)),
            dma((groups,)),
            dma((2,)),
            dma((groups,)),
            dma((groups,)),
            dma((count,)),
            dma((count,)),
        ],
        compiler_params=pltpu.CompilerParams(
            collective_id=0, has_side_effects=True, vmem_limit_bytes=32 << 20
        ),
    )(
        *(
            pltpu.with_memory_space_constraint(x, pltpu.HBM)
            for x in (
                jnp.swapaxes(expert_ids[0], 0, 1),
                jnp.swapaxes(gate_values[0], 0, 1),
                section_grad[0],
                loss_grad,
                down_inputs[0, 0],
            )
        )
    )
    out = pl.pallas_call(
        functools.partial(product_kernel, starts),
        out_shape=jax.ShapeDtypeStruct((width, hidden), bf16),
        in_specs=[VMEM, VMEM],
        out_specs=HBM,
        scratch_shapes=[pltpu.VMEM((width, hidden), bf16), dma((pack * (size // LANES),))],
        compiler_params=pltpu.CompilerParams(vmem_limit_bytes=32 << 20),
    )(rows, weights)
    return out[None]


def solution(mesh):
    in_specs = (
        P("pipe", ("expert", "dp"), None),
        P(("expert", "dp"), None),
        P("pipe", ("expert", "dp"), None),
        P("pipe", ("expert", "dp"), None),
        P("pipe", "dp", None, "expert"),
    )
    out_specs = P("pipe", "dp", "expert")
    return jax.shard_map(local, mesh=mesh, in_specs=in_specs, out_specs=out_specs, check_vma=False)
```

```python
import functools

import jax
import jax.numpy as jnp
from jax import lax
from jax.experimental import pallas as pl
from jax.experimental.pallas import tpu as pltpu
from jax.sharding import PartitionSpec as P

ROUTED = 256
SPLIT = 4
TILE = 16
LANES = 128
VMEM = pl.BlockSpec(memory_space=pltpu.VMEM)
HBM = pl.BlockSpec(memory_space=pltpu.HBM)


def each(count, body):
    if count <= 16:
        for i in range(count):
            body(i)
    else:
        lax.fori_loop(0, count, lambda i, c: (body(i), c)[1], 0)


def dot(a, b, contract):
    return lax.dot_general(a, b, ((contract[0], contract[1]), ((), ())), preferred_element_type=jnp.float32)


def chunk_starts(width, pack):
    size = -(-width // (pack * LANES)) * LANES
    return size, [min(c * size, width - size) for c in range(pack)]


def earlier_tokens(tokens):
    shape = (tokens, tokens)
    earlier = lax.broadcasted_iota(jnp.int32, shape, 0) < lax.broadcasted_iota(jnp.int32, shape, 1)
    return jnp.where(earlier, 1.0, 0.0).astype(jnp.bfloat16)


def make_selector(ids, gates, before, expert, cap):
    tokens = ids.shape[1]
    found = ids == expert
    hit = jnp.sum(jnp.where(found, 1.0, 0.0), axis=0, keepdims=True)
    gate = jnp.sum(jnp.where(found, gates, 0.0), axis=0, keepdims=True)
    hit = jnp.broadcast_to(hit, (TILE, tokens))
    gate = jnp.broadcast_to(gate, (TILE, tokens))
    rank = dot(hit.astype(jnp.bfloat16), before, ((1,), (0,)))
    row = lax.broadcasted_iota(jnp.int32, (TILE, tokens), 0) % cap
    keep = (hit > 0.5) & (rank.astype(jnp.int32) == row)
    return jnp.where(keep, gate, 0.0).astype(jnp.bfloat16)


def gather_kernel(
    cap, ids_hbm, gate_hbm, grad_hbm, loss_hbm, inputs_hbm,
    rows_ref, weights_ref,
    all_inputs_ref, ids_ref, gate_ref, inputs_ref, sel_own, sel_in, grad_v, out,
    small_sem, load_sem, sel_sem, in_send, in_recv, send_sem, recv_sem,
):
    pipes, cols, groups = lax.axis_size("pipe"), lax.axis_size("expert"), lax.axis_size("dp")
    p, e, g = lax.axis_index("pipe"), lax.axis_index("expert"), lax.axis_index("dp")
    experts = cols // SPLIT
    pack = TILE // cap
    width = grad_v.shape[1] // groups
    slots = inputs_ref.shape[0]
    size, starts = chunk_starts(width, pack)
    count = cols * groups
    me = e * groups + g
    after, before = lax.rem(p + 1, pipes), lax.rem(p + pipes - 1, pipes)
    slot = g * cols + e

    def place(pipe, col, group):
        return {"pipe": pipe, "expert": col, "dp": group}

    def load(src, h):
        span = pl.ds(h * width, width)
        return pltpu.make_async_copy(src.at[:, span], grad_v.at[:, span], load_sem.at[h])

    def row_copy(i):
        col, group = i // groups, i % groups
        return pltpu.make_async_remote_copy(
            src_ref=out.at[(col // SPLIT) * groups + group],
            dst_ref=rows_ref.at[slot],
            send_sem=send_sem.at[i],
            recv_sem=recv_sem.at[slot],
            device_id=place(before, col, group),
            device_id_type=pl.DeviceIdType.MESH,
        )

    def selector_copy():
        return pltpu.make_async_remote_copy(
            src_ref=sel_own, dst_ref=sel_in, send_sem=sel_sem.at[0], recv_sem=sel_sem.at[1],
            device_id=place(after, e, g), device_id_type=pl.DeviceIdType.MESH,
        )

    def inputs_copy(group):
        return pltpu.make_async_remote_copy(
            src_ref=inputs_ref, dst_ref=all_inputs_ref.at[g],
            send_sem=in_send.at[group], recv_sem=in_recv.at[g],
            device_id=place(p, e, group), device_id_type=pl.DeviceIdType.MESH,
        )

    def other_group(k):
        return lax.rem(g + 1 + k, groups)

    small = [
        pltpu.make_async_copy(src, dst, small_sem.at[i])
        for i, (src, dst) in enumerate(((ids_hbm, ids_ref), (gate_hbm, gate_ref), (inputs_hbm, inputs_ref)))
    ]
    for copy in small:
        copy.start()

    barrier = pltpu.get_barrier_semaphore()

    def greet(pipe, col, group):
        pl.semaphore_signal(
            barrier, inc=1, device_id=place(pipe, col, group), device_id_type=pl.DeviceIdType.MESH
        )

    greet(before, e, g)
    for k in range(groups - 1):
        greet(p, e, other_group(k))
    each(count, lambda i: greet(after, i // groups, i % groups))

    @pl.when(p == 0)
    def _():
        for h in range(groups):
            load(loss_hbm, h).start()

    @pl.when(p >= 1)
    def _():
        for h in range(groups):
            load(grad_hbm, h).start()

    earlier = earlier_tokens(ids_ref.shape[1])
    for copy in small:
        copy.wait()
    ids = ids_ref[...]
    gates = gate_ref[...].astype(jnp.float32)
    for x in range(experts):
        sel_own[x] = make_selector(ids, gates, earlier, x, cap)
    all_inputs_ref[g] = inputs_ref[...]

    pl.semaphore_wait(barrier, count + groups)
    selector_copy().start()
    for k in range(groups - 1):
        inputs_copy(other_group(k)).start()

    def pick(h):
        for x in range(experts):
            sel = sel_in[x].astype(jnp.float32)
            chunk = lax.broadcasted_iota(jnp.int32, sel.shape, 0) // cap
            total = None
            for c in range(0, pack, 2):
                pair = range(c, min(c + 2, pack))
                parts = [jnp.where(chunk == d, sel, 0.0).astype(jnp.bfloat16) for d in pair]
                values = [grad_v[:, pl.ds(h * width + starts[d], size)] for d in pair]
                term = dot(jnp.concatenate(parts, axis=1), jnp.concatenate(values, axis=0), ((1,), (0,)))
                total = term if total is None else total + term
            out[x * groups + h] = total.astype(jnp.bfloat16)

    selector_copy().wait_recv()
    for h in range(groups):
        load(grad_hbm, h).wait()
        pick(h)
        each(cols, lambda k: row_copy(lax.rem(e + 1 + k, cols) * groups + h).start())

    for k in range(groups - 1):
        group = other_group(k)
        pltpu.make_async_remote_copy(
            src_ref=inputs_ref, dst_ref=all_inputs_ref.at[group],
            send_sem=in_send.at[group], recv_sem=in_recv.at[group],
            device_id=place(p, e, group), device_id_type=pl.DeviceIdType.MESH,
        ).wait()
    weights_ref[...] = spread_inputs(all_inputs_ref[...], cap, count * TILE)

    def arrived(i):
        return pltpu.make_async_remote_copy(
            src_ref=out.at[0], dst_ref=rows_ref.at[i], send_sem=send_sem.at[0], recv_sem=recv_sem.at[i],
            device_id=place(p, e, g), device_id_type=pl.DeviceIdType.MESH,
        )

    each(count, lambda i: arrived(i).wait_recv())
    selector_copy().wait_send()
    each(count, lambda i: row_copy(i).wait_send())


def spread_inputs(inputs, cap, depth):
    groups, slots, hidden = inputs.shape
    inputs = inputs.reshape(groups * slots, hidden)
    r = lax.broadcasted_iota(jnp.int32, (depth, groups * slots), 0)
    s = lax.broadcasted_iota(jnp.int32, (depth, groups * slots), 1)
    spread = jnp.where((r // TILE == s // cap) & (r % cap == s % cap), 1.0, 0.0).astype(jnp.bfloat16)
    wide = dot(spread, inputs, ((1,), (0,)))
    chunk = (lax.broadcasted_iota(jnp.int32, wide.shape, 0) // cap) % (TILE // cap)
    return jnp.concatenate(
        [jnp.where(chunk == c, wide, 0.0).astype(jnp.bfloat16) for c in range(TILE // cap)], axis=1
    )


def product_kernel(starts, rows_ref, weights_ref, out_hbm, out_ref, sem):
    sources, tile, size = rows_ref.shape
    pack = len(starts)
    depth = sources * tile
    hidden = out_ref.shape[1]
    weights = weights_ref[...]
    apart = all(starts[c] == c * size for c in range(pack))
    copies = []

    def flush(first, rows):
        span = pl.ds(first, rows)
        copies.append(pltpu.make_async_copy(out_ref.at[span], out_hbm.at[span], sem.at[len(copies)]))
        copies[-1].start()

    for k in range(size // LANES):
        part = rows_ref[:, :, k * LANES:(k + 1) * LANES].reshape(depth, LANES)
        value = dot(part, weights, ((0,), (0,))).astype(out_ref.dtype)
        for c in range(pack):
            first = starts[c] + k * LANES
            out_ref[first:first + LANES, :] = value[:, c * hidden:(c + 1) * hidden]
            if apart:
                flush(first, LANES)
    if not apart:
        flush(0, out_ref.shape[0])
    for copy in copies:
        copy.wait()


def local(section_grad, loss_grad, expert_ids, gate_values, down_inputs):
    cols, groups = lax.axis_size("expert"), lax.axis_size("dp")
    experts = cols // SPLIT
    tokens, depth = section_grad.shape[1:]
    topk = expert_ids.shape[2]
    cap = tokens * topk // ROUTED
    pack = TILE // cap
    width = depth // groups
    size, starts = chunk_starts(width, pack)
    slots, hidden = down_inputs.shape[2:]
    count = cols * groups
    bf16 = jnp.bfloat16
    dma = pltpu.SemaphoreType.DMA
    rows, weights = pl.pallas_call(
        functools.partial(gather_kernel, cap),
        out_shape=[
            jax.ShapeDtypeStruct((count, TILE, size), bf16),
            jax.ShapeDtypeStruct((count * TILE, pack * hidden), bf16),
        ],
        in_specs=[HBM] * 5,
        out_specs=[VMEM, VMEM],
        scratch_shapes=[
            pltpu.VMEM((groups, slots, hidden), bf16),
            pltpu.VMEM((topk, tokens), expert_ids.dtype),
            pltpu.VMEM((topk, tokens), bf16),
            pltpu.VMEM((slots, hidden), bf16),
            pltpu.VMEM((experts, TILE, tokens), bf16),
            pltpu.VMEM((experts, TILE, tokens), bf16),
            pltpu.VMEM((tokens, depth), bf16),
            pltpu.VMEM((experts * groups, TILE, size), bf16),
            dma((3,)),
            dma((groups,)),
            dma((2,)),
            dma((groups,)),
            dma((groups,)),
            dma((count,)),
            dma((count,)),
        ],
        compiler_params=pltpu.CompilerParams(
            collective_id=0, has_side_effects=True, vmem_limit_bytes=32 << 20
        ),
    )(
        *(
            pltpu.with_memory_space_constraint(x, pltpu.HBM)
            for x in (
                jnp.swapaxes(expert_ids[0], 0, 1),
                jnp.swapaxes(gate_values[0], 0, 1),
                section_grad[0],
                loss_grad,
                down_inputs[0, 0],
            )
        )
    )
    out = pl.pallas_call(
        functools.partial(product_kernel, starts),
        out_shape=jax.ShapeDtypeStruct((width, hidden), bf16),
        in_specs=[VMEM, VMEM],
        out_specs=HBM,
        scratch_shapes=[pltpu.VMEM((width, hidden), bf16), dma((pack * (size // LANES),))],
        compiler_params=pltpu.CompilerParams(vmem_limit_bytes=32 << 20),
    )(rows, weights)
    return out[None]


def solution(mesh):
    in_specs = (
        P("pipe", ("expert", "dp"), None),
        P(("expert", "dp"), None),
        P("pipe", ("expert", "dp"), None),
        P("pipe", ("expert", "dp"), None),
        P("pipe", "dp", None, "expert"),
    )
    out_specs = P("pipe", "dp", "expert")
    return jax.shard_map(local, mesh=mesh, in_specs=in_specs, out_specs=out_specs, check_vma=False)
```
